32 devices in a mesh: cohort: 4 (over y, x), dev: 8 (over z, core).
Axes of the slice: x: 2, y: 2, z: 4, core: 2. Of those that a mesh axis runs over, the one named last changes fastest.
Arguments:
- dosage: bfloat16 [65536, 2048], P(('cohort', 'dev')), may hold values from 0 to 2
- allele_freq: float32 [2048], replicated, may hold values from 0.05 to 0.5
- probes: bfloat16 [2048, 512], replicated, may hold values from -6 to 6
- owner_perm: int32 [2048], replicated, may hold values from 0 to 2047, each once
Outputs:
- projected: float32 [2048, 512], P('dev')
The draws below stay inside these ranges and needn't reach their ends.
Inputs may be any that keep to these rules, and one draw needn't show every extreme that they name: `owner_perm`: each SNP appears exactly once.
All inputs are finite; a program needn't handle non-finite values.
Results may differ from the reference program's by a relative error of at most 0.00044.
Values sent between devices are 32-bit elements; how exact they have to be, the bound alone decides.
A program may use at most 128 MiB of HBM per device.

```python
import jax
import jax.numpy as jnp
from jax import lax

M = 2048
K = 512
SAMPLES = 65536


def block_scale(key, extent, cuts, least, high):
    def one(axis_at, parts):
        draws = jax.random.uniform(jax.random.fold_in(jax.random.fold_in(key, 6), axis_at), (parts,), jnp.float32, least / len(cuts), high / len(cuts))
        return jnp.repeat(jnp.exp(draws), extent[axis_at] // parts).reshape((-1,) + (1,) * (len(extent) - axis_at - 1))

    gain = one(*cuts[0])
    for cut in cuts[1:]:
        gain = gain * one(*cut)
    return gain


def gaussian(rng, extent, width, most, kind=jnp.bfloat16):
    entries = width * jax.random.normal(rng, extent, jnp.float32)
    return jnp.clip(entries, min=-most, max=most).astype(kind)


def setup_inputs(seed: int = 0) -> dict:
    seeds = jax.random.split(jax.random.key(seed), 5)
    dosage = jnp.clip(2.0 * jax.random.uniform(seeds[0], (SAMPLES, M), jnp.float32) ** block_scale(seeds[0], (SAMPLES, M), ((0, 32),), -0.2, 0.2), 0.0, 2.0).astype(jnp.bfloat16)
    allele_freq = jnp.clip(jax.random.uniform(seeds[1], (M,), jnp.float32, 0.05, 0.5), 0.05, 0.5)
    probes = gaussian(seeds[2], (M, K), 1.0, 6.0)
    owner_perm = jax.random.permutation(seeds[3], M).astype(jnp.int32)
    return dict(dosage=dosage, allele_freq=allele_freq, probes=probes, owner_perm=owner_perm)


def reference(dosage, allele_freq, probes, owner_perm):
    mean_dose = 2.0 * allele_freq
    inv_spread = 1.0 / jnp.sqrt(2.0 * allele_freq * (1.0 - allele_freq))
    centered = ((dosage.astype(jnp.float32) - mean_dose[None, :]) * inv_spread[None, :]).astype(jnp.bfloat16)
    sketch = jnp.dot(centered.astype(jnp.float32), probes.astype(jnp.float32), preferred_element_type=jnp.float32)
    gram = jnp.dot(sketch.T, sketch, precision=lax.Precision.HIGHEST)
    lower = jnp.linalg.cholesky(gram)
    basis_t = lax.linalg.triangular_solve(lower, sketch.T, left_side=True, lower=True).astype(jnp.bfloat16)
    full = lax.dot_general(centered.astype(jnp.float32), basis_t.astype(jnp.float32), (((0,), (1,)), ((), ())), preferred_element_type=jnp.float32)
    return jnp.take(full, owner_perm.astype(jnp.int32), axis=0)
```

```python
import jax
import jax.numpy as jnp
from jax import lax
from jax.experimental import pallas as pl
from jax.experimental.pallas import tpu as pltpu
from jax.sharding import PartitionSpec as P

HI = lax.Precision.HIGHEST
NB = 128


def dot(a, b, ca, cb):
    return lax.dot_general(
        a, b, (((ca,), (cb,)), ((), ())), precision=HI, preferred_element_type=jnp.float32
    )


def factor_block(w_ref):
    sub = lax.broadcasted_iota(jnp.int32, (8, 1), 0)
    for p in range(NB // 8):
        lo = 8 * p
        panel = w_ref[lo : lo + 8, :]
        cols = [jnp.broadcast_to(panel[:, lo + j : lo + j + 1], (8, NB)) for j in range(8)]
        for j in range(8):
            r = lax.rsqrt(cols[j][j : j + 1, :])
            m = cols[j] * r
            for i in range(j + 1, 8):
                cols[i] = cols[i] - m * m[i : i + 1, :]
            r2 = jnp.concatenate([r, r], axis=1)
            m2 = jnp.concatenate([m, m], axis=1)
            u = panel[j : j + 1, :] * r2
            panel = jnp.where(sub == j, u, jnp.where(sub > j, panel - m2 * u, panel))
        w_ref[lo : lo + 8, :] = panel
        if lo + 8 < NB:
            base = (lo + 8) // 8 * 8
            left = panel[:, :NB]
            upd = dot(left, panel, 0, 0)
            w_ref[base:, :] = w_ref[base:, :] - upd[base:, :]


def cholesky_loop(a_ref, u_ref, inv_ref, w_ref):
    nb = a_ref.shape[0]
    eye = (
        lax.broadcasted_iota(jnp.int32, (NB, NB), 0) == lax.broadcasted_iota(jnp.int32, (NB, NB), 1)
    ).astype(jnp.float32)

    def step(b, c):
        at = pl.ds(pl.multiple_of(b * NB, NB), NB)
        w_ref[:, :NB] = a_ref[b, :, at]
        w_ref[:, NB:] = eye
        factor_block(w_ref)
        inv = w_ref[:, NB:]
        inv_ref[b] = inv
        u = dot(inv, a_ref[b], 1, 0)
        u_ref[b] = u

        def trail(i, c):
            cols = pl.ds(pl.multiple_of(i * NB, NB), NB)
            a_ref[i] = a_ref[i] - dot(u_ref[b, :, cols], u_ref[b], 0, 0)
            return c

        lax.fori_loop(b + 1, nb, trail, 0)
        return c

    lax.fori_loop(0, nb, step, 0)


def apply(h, u_ref, inv_ref):
    nb = u_ref.shape[0]
    xs = []
    for j in range(nb):
        t = h[:, j * NB : (j + 1) * NB]
        for k in range(j):
            t = t - dot(xs[k], u_ref[k, :, j * NB : (j + 1) * NB], 1, 0)
        xs.append(dot(t, inv_ref[j], 1, 1))
    return jnp.concatenate(xs, axis=1)


def chol_kernel(g_ref, u_ref, inv_ref, a_ref, w_ref):
    nb = u_ref.shape[0]
    for b in range(nb):
        a_ref[b] = g_ref[b * NB : (b + 1) * NB, :]
    cholesky_loop(a_ref, u_ref, inv_ref, w_ref)


def chol(gram):
    k = gram.shape[0]
    nb = k // NB
    return pl.pallas_call(
        chol_kernel,
        out_shape=(
            jax.ShapeDtypeStruct((nb, NB, k), jnp.float32),
            jax.ShapeDtypeStruct((nb, NB, NB), jnp.float32),
        ),
        in_specs=[pl.BlockSpec(memory_space=pltpu.VMEM)],
        out_specs=(pl.BlockSpec(memory_space=pltpu.VMEM),) * 2,
        scratch_shapes=[pltpu.VMEM((nb, NB, k), jnp.float32), pltpu.VMEM((NB, 2 * NB), jnp.float32)],
        compiler_params=pltpu.CompilerParams(vmem_limit_bytes=32 << 20),
        cost_estimate=pl.CostEstimate(flops=10**10, bytes_accessed=4 << 20, transcendentals=0),
    )(gram)


def apply_kernel(h_ref, u_ref, inv_ref, o_ref):
    o_ref[...] = apply(h_ref[...], u_ref, inv_ref)


def apply_inv(h, u, inv):
    return pl.pallas_call(
        apply_kernel,
        out_shape=jax.ShapeDtypeStruct(h.shape, jnp.float32),
        in_specs=[pl.BlockSpec(memory_space=pltpu.VMEM)] * 3,
        out_specs=pl.BlockSpec(memory_space=pltpu.VMEM),
        compiler_params=pltpu.CompilerParams(vmem_limit_bytes=32 << 20),
    )(h, u, inv)


def tdot(a, b):
    return lax.dot_general(a, b, (((0,), (0,)), ((), ())), preferred_element_type=jnp.float32)


def body(dosage, allele_freq, probes, owner_perm):
    mean_dose = 2.0 * allele_freq
    inv_spread = 1.0 / jnp.sqrt(2.0 * allele_freq * (1.0 - allele_freq))
    centered = ((dosage.astype(jnp.float32) - mean_dose[None, :]) * inv_spread[None, :]).astype(
        jnp.bfloat16
    )
    sketch = jnp.dot(centered, probes, preferred_element_type=jnp.float32)
    rounded = lax.reduce_precision(sketch, 8, 7)
    high = rounded.astype(jnp.bfloat16)
    low = (sketch - rounded).astype(jnp.bfloat16)
    cross = tdot(high, low)
    local_gram = tdot(high, high) + (cross + cross.T)
    gram = lax.psum(local_gram, ("cohort", "dev"))
    product = tdot(centered, high) + tdot(centered, low)
    product = jnp.take(product, owner_perm, axis=0)
    owned = lax.psum_scatter(product, "dev", scatter_dimension=0, tiled=True)
    owned = lax.psum(owned, "cohort")
    u, inv = chol(gram)
    return apply_inv(owned, u, inv)


def solution(mesh):
    return jax.shard_map(
        body,
        mesh=mesh,
        in_specs=(P(("cohort", "dev"), None), P(), P(), P()),
        out_specs=P("dev", None),
        check_vma=False,
    )
```

```python
import jax
import jax.numpy as jnp
from jax import lax
from jax.experimental import pallas as pl
from jax.experimental.pallas import tpu as pltpu
from jax.sharding import PartitionSpec as P

HI = lax.Precision.HIGHEST
NB = 128


def dot(a, b, ca, cb):
    return lax.dot_general(
        a, b, (((ca,), (cb,)), ((), ())), precision=HI, preferred_element_type=jnp.float32
    )


def factor_block(w_ref):
    sub = lax.broadcasted_iota(jnp.int32, (8, 1), 0)
    for p in range(NB // 8):
        lo = 8 * p
        panel = w_ref[lo : lo + 8, :]
        cols = [jnp.broadcast_to(panel[:, lo + j : lo + j + 1], (8, NB)) for j in range(8)]
        for j in range(8):
            r = lax.rsqrt(cols[j][j : j + 1, :])
            m = cols[j] * r
            for i in range(j + 1, 8):
                cols[i] = cols[i] - m * m[i : i + 1, :]
            r2 = jnp.concatenate([r, r], axis=1)
            m2 = jnp.concatenate([m, m], axis=1)
            u = panel[j : j + 1, :] * r2
            panel = jnp.where(sub == j, u, jnp.where(sub > j, panel - m2 * u, panel))
        w_ref[lo : lo + 8, :] = panel
        if lo + 8 < NB:
            base = (lo + 8) // 8 * 8
            left = panel[:, :NB]
            upd = dot(left, panel, 0, 0)
            w_ref[base:, :] = w_ref[base:, :] - upd[base:, :]


def cholesky_loop(a_ref, u_ref, inv_ref, w_ref, between=None):
    nb = a_ref.shape[0]
    eye = (
        lax.broadcasted_iota(jnp.int32, (NB, NB), 0) == lax.broadcasted_iota(jnp.int32, (NB, NB), 1)
    ).astype(jnp.float32)

    def step(b, c):
        if between is not None:
            pl.when(b == nb // 2)(between)
        at = pl.ds(pl.multiple_of(b * NB, NB), NB)
        w_ref[:, :NB] = a_ref[b, :, at]
        w_ref[:, NB:] = eye
        factor_block(w_ref)
        inv = w_ref[:, NB:]
        inv_ref[b] = inv
        u = dot(inv, a_ref[b], 1, 0)
        u_ref[b] = u

        def trail(i, c):
            cols = pl.ds(pl.multiple_of(i * NB, NB), NB)
            a_ref[i] = a_ref[i] - dot(u_ref[b, :, cols], u_ref[b], 0, 0)
            return c

        lax.fori_loop(b + 1, nb, trail, 0)
        return c

    lax.fori_loop(0, nb, step, 0)


def apply(h, u_ref, inv_ref):
    nb = u_ref.shape[0]
    xs = []
    for j in range(nb):
        t = h[:, j * NB : (j + 1) * NB]
        for k in range(j):
            t = t - dot(xs[k], u_ref[k, :, j * NB : (j + 1) * NB], 1, 0)
        xs.append(dot(t, inv_ref[j], 1, 1))
    return jnp.concatenate(xs, axis=1)


MESH = pl.DeviceIdType.MESH


def kernel(shape, g_ref, h_ref, o_ref, gc, gacc, gq, gz, gzb, gout, hc, hacc, hq, hz, hzb, a_ref, u_ref, inv_ref, w_ref, send, recv):
    groups, lanes_z = shape
    coh, dev = lax.axis_index("cohort"), lax.axis_index("dev")
    core, z = lax.rem(dev, 2), dev // 2
    half, rq, rz = gc.shape[0], gq.shape[1], gzb.shape[1]

    def at_cohort(k):
        return lax.rem(coh + k, groups)

    def at_z(k):
        return lax.rem(z + k, lanes_z)

    core_peer = (coh, 2 * z + 1 - core)
    cohort_peers = [(at_cohort(k), dev) for k in range(1, groups)]
    z_peers = [(coh, 2 * at_z(k) + core) for k in range(1, lanes_z)]
    used = [0]

    def copy(src, dst, peer):
        n = used[0]
        used[0] += 1
        return pltpu.make_async_remote_copy(
            src_ref=src, dst_ref=dst, send_sem=send.at[n], recv_sem=recv.at[n],
            device_id=peer, device_id_type=MESH,
        )

    def start(copies):
        for c in copies:
            c.start()

    def wait(copies):
        for c in copies:
            c.wait()

    def rows(at, size):
        return pl.ds(pl.multiple_of(at * size, 8), size)

    barrier = pltpu.get_barrier_semaphore()
    peers = [core_peer] + cohort_peers + z_peers
    for peer in peers:
        pl.semaphore_signal(barrier, inc=1, device_id=peer, device_id_type=MESH)
    pl.semaphore_wait(barrier, len(peers))

    g1 = [copy(g_ref.at[rows(1 - core, half)], gc, core_peer)]
    h1 = [copy(h_ref.at[:, 1 - core], hc, core_peer)]
    start(g1)
    start(h1)
    wait(g1)
    gacc[...] = g_ref[rows(core, half), :] + gc[...]
    g2 = [copy(gacc.at[rows(at_cohort(k), rq)], gq.at[k - 1], cohort_peers[k - 1]) for k in range(1, groups)]
    start(g2)
    wait(g2)
    total = gacc[rows(coh, rq), :]
    for k in range(groups - 1):
        total = total + gq[k]
    gz[...] = total
    g3 = [copy(gz.at[rows(at_z(k), rz)], gzb.at[k - 1], z_peers[k - 1]) for k in range(1, lanes_z)]
    start(g3)

    wait(h1)

    def add_core(i, c):
        for q in range(groups):
            hacc[q, i] = h_ref[i, core, q] + hc[i, q]
        return c

    lax.fori_loop(0, lanes_z, add_core, 0)

    wait(g3)
    total = gz[rows(z, rz), :]
    for k in range(lanes_z - 1):
        total = total + gzb[k]
    own_q = core * groups + coh
    own = rows(own_q * lanes_z + z, rz)
    gout[own, :] = total
    g4 = [copy(gout.at[own], gout.at[own], peer) for peer in z_peers]
    start(g4)
    wait(g4)
    own = rows(own_q, rq)
    g5 = [copy(gout.at[own], gout.at[own], peer) for peer in cohort_peers]
    start(g5)
    h2 = [copy(hacc.at[at_cohort(k)], hq.at[k - 1], cohort_peers[k - 1]) for k in range(1, groups)]
    start(h2)
    wait(g5)
    own = rows(core, half)
    g6 = [copy(gout.at[own], gout.at[own], core_peer)]
    start(g6)
    wait(g6)

    nb = a_ref.shape[0]
    n = 0
    for b in range(nb):
        for c in range(nb):
            cols = slice(c * NB, (c + 1) * NB)
            if c < b:
                a_ref[b, :, cols] = jnp.zeros((NB, NB), jnp.float32)
            else:
                a_ref[b, :, cols] = gout[n * NB : (n + 1) * NB, :]
                n += 1

    h3 = [copy(hz.at[at_z(k)], hzb.at[k - 1], z_peers[k - 1]) for k in range(1, lanes_z)]

    def between():
        wait(h2)

        def add_cohort(i, c):
            t = hacc[coh, i]
            for k in range(groups - 1):
                t = t + hq[k, i]
            hz[i] = t
            return c

        lax.fori_loop(0, lanes_z, add_cohort, 0)
        start(h3)

    cholesky_loop(a_ref, u_ref, inv_ref, w_ref, between)
    wait(h3)
    h = hz[z]
    for k in range(lanes_z - 1):
        h = h + hzb[k]
    rc = h.shape[0]
    own = rows(coh, rc)
    o_ref[own, :] = apply(h, u_ref, inv_ref)
    h4 = [copy(o_ref.at[own], o_ref.at[own], peer) for peer in cohort_peers]
    start(h4)
    wait(h4)


def reduce_and_apply(gram, product, groups, devs):
    k = gram.shape[0]
    nb = k // NB
    m = product.shape[0]
    z = devs // 2
    r = m // devs
    rc = r // groups
    blocks = [gram[b * NB : (b + 1) * NB, c * NB : (c + 1) * NB] for b in range(nb) for c in range(b, nb)]
    count = len(blocks) * NB
    unit = 8 * groups * devs
    total = -(-count // unit) * unit
    if total > count:
        blocks.append(jnp.zeros((total - count, NB), jnp.float32))
    packed = jnp.concatenate(blocks, axis=0)
    product = product.reshape(z, 2, groups, rc, k)
    half = total // 2
    rq = half // groups
    rz = rq // z
    copies = 3 + 4 * (groups - 1) + 3 * (z - 1)
    f32 = jnp.float32
    return pl.pallas_call(
        lambda *refs: kernel((groups, z), *refs),
        out_shape=jax.ShapeDtypeStruct((r, k), f32),
        in_specs=[pl.BlockSpec(memory_space=pltpu.VMEM)] * 2,
        out_specs=pl.BlockSpec(memory_space=pltpu.VMEM),
        scratch_shapes=[
            pltpu.VMEM((half, NB), f32),
            pltpu.VMEM((half, NB), f32),
            pltpu.VMEM((groups - 1, rq, NB), f32),
            pltpu.VMEM((rq, NB), f32),
            pltpu.VMEM((z - 1, rz, NB), f32),
            pltpu.VMEM((total, NB), f32),
            pltpu.VMEM((z, groups, rc, k), f32),
            pltpu.VMEM((groups, z, rc, k), f32),
            pltpu.VMEM((groups - 1, z, rc, k), f32),
            pltpu.VMEM((z, rc, k), f32),
            pltpu.VMEM((z - 1, rc, k), f32),
            pltpu.VMEM((nb, NB, k), f32),
            pltpu.VMEM((nb, NB, k), f32),
            pltpu.VMEM((nb, NB, NB), f32),
            pltpu.VMEM((NB, 2 * NB), f32),
            pltpu.SemaphoreType.DMA((copies,)),
            pltpu.SemaphoreType.DMA((copies,)),
        ],
        compiler_params=pltpu.CompilerParams(
            vmem_limit_bytes=40 << 20, collective_id=0, has_side_effects=True
        ),
    )(packed, product)


def tdot(a, b):
    return lax.dot_general(a, b, (((0,), (0,)), ((), ())), preferred_element_type=jnp.float32)


def body(groups, devs, dosage, allele_freq, probes, owner_perm):
    mean_dose = 2.0 * allele_freq
    inv_spread = 1.0 / jnp.sqrt(2.0 * allele_freq * (1.0 - allele_freq))
    centered = ((dosage.astype(jnp.float32) - mean_dose[None, :]) * inv_spread[None, :]).astype(
        jnp.bfloat16
    )
    sketch = jnp.dot(centered, probes, preferred_element_type=jnp.float32)
    rounded = lax.reduce_precision(sketch, 8, 7)
    high = rounded.astype(jnp.bfloat16)
    low = (sketch - rounded).astype(jnp.bfloat16)
    cross = tdot(high, low)
    local_gram = tdot(high, high) + (cross + cross.T)
    product = tdot(centered, high) + tdot(centered, low)
    product = jnp.take(product, owner_perm, axis=0)
    return reduce_and_apply(local_gram, product, groups, devs)


def solution(mesh):
    return jax.shard_map(
        lambda *args: body(mesh.shape["cohort"], mesh.shape["dev"], *args),
        mesh=mesh,
        in_specs=(P(("cohort", "dev"), None), P(), P(), P()),
        out_specs=P("dev", None),
        check_vma=False,
    )
```

```python
import jax
import jax.numpy as jnp
from jax import lax
from jax.experimental import pallas as pl
from jax.experimental.pallas import tpu as pltpu
from jax.sharding import PartitionSpec as P

HI = lax.Precision.HIGHEST
NB = 128


def dot(a, b, ca, cb):
    return lax.dot_general(
        a, b, (((ca,), (cb,)), ((), ())), precision=HI, preferred_element_type=jnp.float32
    )


def factor_block(w_ref):
    sub = lax.broadcasted_iota(jnp.int32, (8, 1), 0)
    for p in range(NB // 8):
        lo = 8 * p
        panel = w_ref[lo : lo + 8, :]
        cols = [jnp.broadcast_to(panel[:, lo + j : lo + j + 1], (8, NB)) for j in range(8)]
        for j in range(8):
            r = lax.rsqrt(cols[j][j : j + 1, :])
            m = cols[j] * r
            for i in range(j + 1, 8):
                cols[i] = cols[i] - m * m[i : i + 1, :]
            r2 = jnp.concatenate([r, r], axis=1)
            m2 = jnp.concatenate([m, m], axis=1)
            u = panel[j : j + 1, :] * r2
            panel = jnp.where(sub == j, u, jnp.where(sub > j, panel - m2 * u, panel))
        w_ref[lo : lo + 8, :] = panel
        if lo + 8 < NB:
            base = (lo + 8) // 8 * 8
            left = panel[:, :NB]
            upd = dot(left, panel, 0, 0)
            w_ref[base:, :] = w_ref[base:, :] - upd[base:, :]


def cholesky_loop(a_ref, u_ref, inv_ref, w_ref, between=None):
    nb = a_ref.shape[0]
    eye = (
        lax.broadcasted_iota(jnp.int32, (NB, NB), 0) == lax.broadcasted_iota(jnp.int32, (NB, NB), 1)
    ).astype(jnp.float32)

    def step(b, c):
        for at_block, act in (between or {}).items():
            pl.when(b == at_block)(act)
        at = pl.ds(pl.multiple_of(b * NB, NB), NB)
        w_ref[:, :NB] = a_ref[b, :, at]
        w_ref[:, NB:] = eye
        factor_block(w_ref)
        inv = w_ref[:, NB:]
        inv_ref[b] = inv
        u = dot(inv, a_ref[b], 1, 0)
        u_ref[b] = u

        def trail(i, c):
            cols = pl.ds(pl.multiple_of(i * NB, NB), NB)
            a_ref[i] = a_ref[i] - dot(u_ref[b, :, cols], u_ref[b], 0, 0)
            return c

        lax.fori_loop(b + 1, nb, trail, 0)
        return c

    lax.fori_loop(0, nb, step, 0)


def apply(h, u_ref, inv_ref):
    nb = u_ref.shape[0]
    xs = []
    for j in range(nb):
        t = h[:, j * NB : (j + 1) * NB]
        for k in range(j):
            t = t - dot(xs[k], u_ref[k, :, j * NB : (j + 1) * NB], 1, 0)
        xs.append(dot(t, inv_ref[j], 1, 1))
    return jnp.concatenate(xs, axis=1)


MESH = pl.DeviceIdType.MESH


def kernel(shape, perm_ref, g_ref, c_hbm, s_hbm, o_ref, c_ref, s_ref, hv, h_ref, local, gc, gacc, gq, gz, gzb, gout, hc, hacc, hq, hz, hzb, a_ref, u_ref, inv_ref, w_ref, send, recv):
    groups, lanes_z = shape
    coh, dev = lax.axis_index("cohort"), lax.axis_index("dev")
    core, z = lax.rem(dev, 2), dev // 2
    half, rq, rz = gc.shape[0], gq.shape[1], gzb.shape[1]

    def at_cohort(k):
        return lax.rem(coh + k, groups)

    def at_z(k):
        return lax.rem(z + k, lanes_z)

    core_peer = (coh, 2 * z + 1 - core)
    cohort_peers = [(at_cohort(k), dev) for k in range(1, groups)]
    z_peers = [(coh, 2 * at_z(k) + core) for k in range(1, lanes_z)]
    used = [0]

    def copy(src, dst, peer):
        n = used[0]
        used[0] += 1
        return pltpu.make_async_remote_copy(
            src_ref=src, dst_ref=dst, send_sem=send.at[n], recv_sem=recv.at[n],
            device_id=peer, device_id_type=MESH,
        )

    def start(copies):
        for c in copies:
            c.start()

    def wait(copies):
        for c in copies:
            c.wait()

    def rows(at, size):
        return pl.ds(pl.multiple_of(at * size, 8), size)

    loads = [
        pltpu.make_async_copy(c_hbm, c_ref, local.at[0]),
        pltpu.make_async_copy(s_hbm, s_ref, local.at[1]),
    ]
    start(loads)
    chunk = NB * 2
    count = c_ref.shape[1] // chunk
    k_cols = o_ref.shape[1]

    def multiply(first, last):
        def one(i, c):
            at = pl.ds(pl.multiple_of(i * chunk, chunk), chunk)
            both = lax.dot_general(
                c_ref[:, at], s_ref[...], (((0,), (0,)), ((), ())), preferred_element_type=jnp.float32
            )
            hv[at, :] = both[:, :k_cols] + both[:, k_cols:]
            return c

        lax.fori_loop(first, last, one, 0)

    barrier = pltpu.get_barrier_semaphore()
    peers = [core_peer] + cohort_peers + z_peers
    for peer in peers:
        pl.semaphore_signal(barrier, inc=1, device_id=peer, device_id_type=MESH)
    pl.semaphore_wait(barrier, len(peers))

    g1 = [copy(g_ref.at[rows(1 - core, half)], gc, core_peer)]
    h1 = [copy(h_ref.at[:, 1 - core], hc, core_peer)]
    start(g1)
    wait(loads)
    multiply(0, count // 8)
    wait(g1)
    gacc[...] = g_ref[rows(core, half), :] + gc[...]
    g2 = [copy(gacc.at[rows(at_cohort(k), rq)], gq.at[k - 1], cohort_peers[k - 1]) for k in range(1, groups)]
    start(g2)
    multiply(count // 8, 3 * count // 8)
    wait(g2)
    total = gacc[rows(coh, rq), :]
    for k in range(groups - 1):
        total = total + gq[k]
    gz[...] = total
    g3 = [copy(gz.at[rows(at_z(k), rz)], gzb.at[k - 1], z_peers[k - 1]) for k in range(1, lanes_z)]
    start(g3)

    multiply(3 * count // 8, count // 2)
    wait(g3)
    total = gz[rows(z, rz), :]
    for k in range(lanes_z - 1):
        total = total + gzb[k]
    own_q = core * groups + coh
    own = rows(own_q * lanes_z + z, rz)
    gout[own, :] = total
    g4 = [copy(gout.at[own], gout.at[own], peer) for peer in z_peers]
    start(g4)
    multiply(count // 2, 5 * count // 8)
    wait(g4)
    own = rows(own_q, rq)
    g5 = [copy(gout.at[own], gout.at[own], peer) for peer in cohort_peers]
    start(g5)
    multiply(5 * count // 8, count)
    wait(g5)
    own = rows(core, half)
    g6 = [copy(gout.at[own], gout.at[own], core_peer)]
    start(g6)

    rc = h_ref.shape[3]

    def owner(i, c):
        iz, i1 = i // (2 * groups), lax.rem(i, 2 * groups)
        ic, iq = i1 // groups, lax.rem(i1, groups)

        def eight(j, c):
            for t in range(8):
                row = perm_ref[i * rc + j * 8 + t]
                h_ref[iz, ic, iq, pl.ds(j * 8 + t, 1), :] = hv[pl.ds(row, 1), :]
            return c

        lax.fori_loop(0, rc // 8, eight, 0)
        return c

    lax.fori_loop(0, lanes_z * 2 * groups, owner, 0)
    start(h1)
    wait(g6)
    h2 = [copy(hacc.at[at_cohort(k)], hq.at[k - 1], cohort_peers[k - 1]) for k in range(1, groups)]

    nb = a_ref.shape[0]
    n = 0
    for b in range(nb):
        for c in range(nb):
            cols = slice(c * NB, (c + 1) * NB)
            if c < b:
                a_ref[b, :, cols] = jnp.zeros((NB, NB), jnp.float32)
            else:
                a_ref[b, :, cols] = gout[n * NB : (n + 1) * NB, :]
                n += 1

    h3 = [copy(hz.at[at_z(k)], hzb.at[k - 1], z_peers[k - 1]) for k in range(1, lanes_z)]

    def first():
        wait(h1)

        def add_core(i, c):
            for q in range(groups):
                hacc[q, i] = h_ref[i, core, q] + hc[i, q]
            return c

        lax.fori_loop(0, lanes_z, add_core, 0)
        start(h2)

    def second():
        wait(h2)

        def add_cohort(i, c):
            t = hacc[coh, i]
            for k in range(groups - 1):
                t = t + hq[k, i]
            hz[i] = t
            return c

        lax.fori_loop(0, lanes_z, add_cohort, 0)
        start(h3)

    cholesky_loop(a_ref, u_ref, inv_ref, w_ref, {1: first, nb - 1: second})
    wait(h3)
    h = hz[z]
    for k in range(lanes_z - 1):
        h = h + hzb[k]
    own = rows(coh, rc)
    o_ref[own, :] = apply(h, u_ref, inv_ref)
    h4 = [copy(o_ref.at[own], o_ref.at[own], peer) for peer in cohort_peers]
    start(h4)
    wait(h4)


def reduce_and_apply(gram, centered, parts, owner_perm, groups, devs):
    k = gram.shape[0]
    nb = k // NB
    m = centered.shape[1]
    z = devs // 2
    r = m // devs
    rc = r // groups
    blocks = [gram[b * NB : (b + 1) * NB, c * NB : (c + 1) * NB] for b in range(nb) for c in range(b, nb)]
    count = len(blocks) * NB
    unit = 8 * groups * devs
    total = -(-count // unit) * unit
    if total > count:
        blocks.append(jnp.zeros((total - count, NB), jnp.float32))
    packed = jnp.concatenate(blocks, axis=0)
    half = total // 2
    rq = half // groups
    rz = rq // z
    copies = 3 + 4 * (groups - 1) + 3 * (z - 1)
    f32 = jnp.float32
    return pl.pallas_call(
        lambda *refs: kernel((groups, z), *refs),
        out_shape=jax.ShapeDtypeStruct((r, k), f32),
        in_specs=[
            pl.BlockSpec(memory_space=pltpu.SMEM),
            pl.BlockSpec(memory_space=pltpu.VMEM),
            pl.BlockSpec(memory_space=pl.ANY),
            pl.BlockSpec(memory_space=pl.ANY),
        ],
        out_specs=pl.BlockSpec(memory_space=pltpu.VMEM),
        scratch_shapes=[
            pltpu.VMEM(centered.shape, centered.dtype),
            pltpu.VMEM(parts.shape, parts.dtype),
            pltpu.VMEM((m, k), f32),
            pltpu.VMEM((z, 2, groups, rc, k), f32),
            pltpu.SemaphoreType.DMA((2,)),
            pltpu.VMEM((half, NB), f32),
            pltpu.VMEM((half, NB), f32),
            pltpu.VMEM((groups - 1, rq, NB), f32),
            pltpu.VMEM((rq, NB), f32),
            pltpu.VMEM((z - 1, rz, NB), f32),
            pltpu.VMEM((total, NB), f32),
            pltpu.VMEM((z, groups, rc, k), f32),
            pltpu.VMEM((groups, z, rc, k), f32),
            pltpu.VMEM((groups - 1, z, rc, k), f32),
            pltpu.VMEM((z, rc, k), f32),
            pltpu.VMEM((z - 1, rc, k), f32),
            pltpu.VMEM((nb, NB, k), f32),
            pltpu.VMEM((nb, NB, k), f32),
            pltpu.VMEM((nb, NB, NB), f32),
            pltpu.VMEM((NB, 2 * NB), f32),
            pltpu.SemaphoreType.DMA((copies,)),
            pltpu.SemaphoreType.DMA((copies,)),
        ],
        compiler_params=pltpu.CompilerParams(
            vmem_limit_bytes=56 << 20, collective_id=0, has_side_effects=True
        ),
    )(owner_perm, packed, centered, parts)


def tdot(a, b):
    return lax.dot_general(a, b, (((0,), (0,)), ((), ())), preferred_element_type=jnp.float32)


def body(groups, devs, dosage, allele_freq, probes, owner_perm):
    mean_dose = 2.0 * allele_freq
    inv_spread = 1.0 / jnp.sqrt(2.0 * allele_freq * (1.0 - allele_freq))
    centered = ((dosage.astype(jnp.float32) - mean_dose[None, :]) * inv_spread[None, :]).astype(
        jnp.bfloat16
    )
    sketch = jnp.dot(centered, probes, preferred_element_type=jnp.float32)
    rounded = lax.reduce_precision(sketch, 8, 7)
    high = rounded.astype(jnp.bfloat16)
    low = (sketch - rounded).astype(jnp.bfloat16)
    local_gram = tdot(high, high) + (tdot(high, low) + tdot(low, high))
    parts = jnp.concatenate([high, low], axis=1)
    return reduce_and_apply(local_gram, centered, parts, owner_perm, groups, devs)


def solution(mesh):
    return jax.shard_map(
        lambda *args: body(mesh.shape["cohort"], mesh.shape["dev"], *args),
        mesh=mesh,
        in_specs=(P(("cohort", "dev"), None), P(), P(), P()),
        out_specs=P("dev", None),
        check_vma=False,
    )
```

```python
import jax
import jax.numpy as jnp
from jax import lax
from jax.experimental import pallas as pl
from jax.experimental.pallas import tpu as pltpu
from jax.sharding import PartitionSpec as P

HI = lax.Precision.HIGHEST
NB = 128


def dot(a, b, ca, cb):
    return lax.dot_general(
        a, b, (((ca,), (cb,)), ((), ())), precision=HI, preferred_element_type=jnp.float32
    )


def split(x):
    high = x.astype(jnp.bfloat16).astype(jnp.float32)
    mid = (x - high).astype(jnp.bfloat16).astype(jnp.float32)
    return high, mid, x - high - mid


def dot_parts(a, b):
    ah, am, al = split(a)
    bh, bm, bl = split(b)
    left = jnp.concatenate([ah, ah, am, ah, am, al], axis=0).astype(jnp.bfloat16)
    right = jnp.concatenate([bh, bm, bh, bl, bm, bh], axis=0).astype(jnp.bfloat16)
    return lax.dot_general(left, right, (((0,), (0,)), ((), ())), preferred_element_type=jnp.float32)


def factor_block(w_ref):
    sub = lax.broadcasted_iota(jnp.int32, (8, 1), 0)
    for p in range(NB // 8):
        lo = 8 * p
        panel = w_ref[lo : lo + 8, :]
        cols = [jnp.broadcast_to(panel[:, lo + j : lo + j + 1], (8, NB)) for j in range(8)]
        for j in range(8):
            r = lax.rsqrt(cols[j][j : j + 1, :])
            m = cols[j] * r
            for i in range(j + 1, 8):
                cols[i] = cols[i] - m * m[i : i + 1, :]
            r2 = jnp.concatenate([r, r], axis=1)
            m2 = jnp.concatenate([m, m], axis=1)
            u = panel[j : j + 1, :] * r2
            panel = jnp.where(sub == j, u, jnp.where(sub > j, panel - m2 * u, panel))
        w_ref[lo : lo + 8, :] = panel
        if lo + 8 < NB:
            base = (lo + 8) // 8 * 8
            left = panel[:, :NB]
            upd = dot_parts(left, panel)
            w_ref[base:, :] = w_ref[base:, :] - upd[base:, :]


def cholesky_loop(a_ref, u_ref, inv_ref, w_ref, between=None):
    nb = a_ref.shape[0]
    eye = (
        lax.broadcasted_iota(jnp.int32, (NB, NB), 0) == lax.broadcasted_iota(jnp.int32, (NB, NB), 1)
    ).astype(jnp.float32)

    def step(b, c):
        for at_block, act in (between or {}).items():
            pl.when(b == at_block)(act)
        at = pl.ds(pl.multiple_of(b * NB, NB), NB)
        w_ref[:, :NB] = a_ref[b, :, at]
        w_ref[:, NB:] = eye
        factor_block(w_ref)
        inv = w_ref[:, NB:]
        inv_ref[b] = inv
        u = dot(inv, a_ref[b], 1, 0)
        u_ref[b] = u

        def trail(i, c):
            cols = pl.ds(pl.multiple_of(i * NB, NB), NB)
            a_ref[i] = a_ref[i] - dot(u_ref[b, :, cols], u_ref[b], 0, 0)
            return c

        lax.fori_loop(b + 1, nb, trail, 0)
        return c

    lax.fori_loop(0, nb, step, 0)


def apply(h, u_ref, inv_ref):
    nb = u_ref.shape[0]
    xs = []
    for j in range(nb):
        t = h[:, j * NB : (j + 1) * NB]
        for k in range(j):
            t = t - dot(xs[k], u_ref[k, :, j * NB : (j + 1) * NB], 1, 0)
        xs.append(dot(t, inv_ref[j], 1, 1))
    return jnp.concatenate(xs, axis=1)


MESH = pl.DeviceIdType.MESH


def kernel(shape, perm_ref, g_ref, c_hbm, s_hbm, o_ref, c_ref, s_ref, hv, h_ref, local, gc, gacc, gq, gz, gzb, gout, hc, hacc, hq, hz, hzb, a_ref, u_ref, inv_ref, w_ref, send, recv):
    groups, lanes_z = shape
    coh, dev = lax.axis_index("cohort"), lax.axis_index("dev")
    core, z = lax.rem(dev, 2), dev // 2
    half, rq, rz = gc.shape[0], gq.shape[1], gzb.shape[1]

    def at_cohort(k):
        return lax.rem(coh + k, groups)

    def at_z(k):
        return lax.rem(z + k, lanes_z)

    core_peer = (coh, 2 * z + 1 - core)
    cohort_peers = [(at_cohort(k), dev) for k in range(1, groups)]
    z_peers = [(coh, 2 * at_z(k) + core) for k in range(1, lanes_z)]
    used = [0]

    def copy(src, dst, peer):
        n = used[0]
        used[0] += 1
        return pltpu.make_async_remote_copy(
            src_ref=src, dst_ref=dst, send_sem=send.at[n], recv_sem=recv.at[n],
            device_id=peer, device_id_type=MESH,
        )

    def start(copies):
        for c in copies:
            c.start()

    def wait(copies):
        for c in copies:
            c.wait()

    def rows(at, size):
        return pl.ds(pl.multiple_of(at * size, 8), size)

    loads = [
        pltpu.make_async_copy(c_hbm, c_ref, local.at[0]),
        pltpu.make_async_copy(s_hbm, s_ref, local.at[1]),
    ]
    start(loads)
    chunk = NB * 2
    count = c_ref.shape[1] // chunk
    k_cols = o_ref.shape[1]

    def multiply(first, last):
        def one(i, c):
            at = pl.ds(pl.multiple_of(i * chunk, chunk), chunk)
            both = lax.dot_general(
                c_ref[:, at], s_ref[...], (((0,), (0,)), ((), ())), preferred_element_type=jnp.float32
            )
            hv[at, :] = both[:, :k_cols] + both[:, k_cols:]
            return c

        lax.fori_loop(first, last, one, 0)

    barrier = pltpu.get_barrier_semaphore()
    peers = [core_peer] + cohort_peers + z_peers
    for peer in peers:
        pl.semaphore_signal(barrier, inc=1, device_id=peer, device_id_type=MESH)
    pl.semaphore_wait(barrier, len(peers))

    g1 = [copy(g_ref.at[rows(1 - core, half)], gc, core_peer)]
    h1 = [copy(h_ref.at[:, 1 - core], hc, core_peer)]
    start(g1)
    wait(loads)
    multiply(0, count // 8)
    wait(g1)
    gacc[...] = g_ref[rows(core, half), :] + gc[...]
    g2 = [copy(gacc.at[rows(at_cohort(k), rq)], gq.at[k - 1], cohort_peers[k - 1]) for k in range(1, groups)]
    start(g2)
    multiply(count // 8, 3 * count // 8)
    wait(g2)
    total = gacc[rows(coh, rq), :]
    for k in range(groups - 1):
        total = total + gq[k]
    gz[...] = total
    g3 = [copy(gz.at[rows(at_z(k), rz)], gzb.at[k - 1], z_peers[k - 1]) for k in range(1, lanes_z)]
    start(g3)

    multiply(3 * count // 8, count // 2)
    wait(g3)
    total = gz[rows(z, rz), :]
    for k in range(lanes_z - 1):
        total = total + gzb[k]
    own_q = core * groups + coh
    own = rows(own_q * lanes_z + z, rz)
    gout[own, :] = total
    g4 = [copy(gout.at[own], gout.at[own], peer) for peer in z_peers]
    start(g4)
    multiply(count // 2, 5 * count // 8)
    wait(g4)
    own = rows(own_q, rq)
    g5 = [copy(gout.at[own], gout.at[own], peer) for peer in cohort_peers]
    start(g5)
    multiply(5 * count // 8, count)
    wait(g5)
    own = rows(core, half)
    g6 = [copy(gout.at[own], gout.at[own], core_peer)]
    start(g6)

    rc = h_ref.shape[3]

    def owner(i, c):
        iz, i1 = i // (2 * groups), lax.rem(i, 2 * groups)
        ic, iq = i1 // groups, lax.rem(i1, groups)

        def eight(j, c):
            for t in range(8):
                row = perm_ref[i * rc + j * 8 + t]
                h_ref[iz, ic, iq, pl.ds(j * 8 + t, 1), :] = hv[pl.ds(row, 1), :]
            return c

        lax.fori_loop(0, rc // 8, eight, 0)
        return c

    lax.fori_loop(0, lanes_z * 2 * groups, owner, 0)
    start(h1)
    wait(g6)
    h2 = [copy(hacc.at[at_cohort(k)], hq.at[k - 1], cohort_peers[k - 1]) for k in range(1, groups)]

    nb = a_ref.shape[0]
    n = 0
    for b in range(nb):
        for c in range(nb):
            cols = slice(c * NB, (c + 1) * NB)
            if c < b:
                a_ref[b, :, cols] = jnp.zeros((NB, NB), jnp.float32)
            else:
                a_ref[b, :, cols] = gout[n * NB : (n + 1) * NB, :]
                n += 1

    h3 = [copy(hz.at[at_z(k)], hzb.at[k - 1], z_peers[k - 1]) for k in range(1, lanes_z)]

    def first():
        wait(h1)

        def add_core(i, c):
            for q in range(groups):
                hacc[q, i] = h_ref[i, core, q] + hc[i, q]
            return c

        lax.fori_loop(0, lanes_z, add_core, 0)
        start(h2)

    def second():
        wait(h2)

        def add_cohort(i, c):
            t = hacc[coh, i]
            for k in range(groups - 1):
                t = t + hq[k, i]
            hz[i] = t
            return c

        lax.fori_loop(0, lanes_z, add_cohort, 0)
        start(h3)

    cholesky_loop(a_ref, u_ref, inv_ref, w_ref, {1: first, nb - 1: second})
    wait(h3)
    h = hz[z]
    for k in range(lanes_z - 1):
        h = h + hzb[k]
    own = rows(coh, rc)
    o_ref[own, :] = apply(h, u_ref, inv_ref)
    h4 = [copy(o_ref.at[own], o_ref.at[own], peer) for peer in cohort_peers]
    start(h4)
    wait(h4)


def reduce_and_apply(gram, centered, parts, owner_perm, groups, devs):
    k = gram.shape[0]
    nb = k // NB
    m = centered.shape[1]
    z = devs // 2
    r = m // devs
    rc = r // groups
    blocks = [gram[b * NB : (b + 1) * NB, c * NB : (c + 1) * NB] for b in range(nb) for c in range(b, nb)]
    count = len(blocks) * NB
    unit = 8 * groups * devs
    total = -(-count // unit) * unit
    if total > count:
        blocks.append(jnp.zeros((total - count, NB), jnp.float32))
    packed = jnp.concatenate(blocks, axis=0)
    half = total // 2
    rq = half // groups
    rz = rq // z
    copies = 3 + 4 * (groups - 1) + 3 * (z - 1)
    f32 = jnp.float32
    return pl.pallas_call(
        lambda *refs: kernel((groups, z), *refs),
        out_shape=jax.ShapeDtypeStruct((r, k), f32),
        in_specs=[
            pl.BlockSpec(memory_space=pltpu.SMEM),
            pl.BlockSpec(memory_space=pltpu.VMEM),
            pl.BlockSpec(memory_space=pl.ANY),
            pl.BlockSpec(memory_space=pl.ANY),
        ],
        out_specs=pl.BlockSpec(memory_space=pltpu.VMEM),
        scratch_shapes=[
            pltpu.VMEM(centered.shape, centered.dtype),
            pltpu.VMEM(parts.shape, parts.dtype),
            pltpu.VMEM((m, k), f32),
            pltpu.VMEM((z, 2, groups, rc, k), f32),
            pltpu.SemaphoreType.DMA((2,)),
            pltpu.VMEM((half, NB), f32),
            pltpu.VMEM((half, NB), f32),
            pltpu.VMEM((groups - 1, rq, NB), f32),
            pltpu.VMEM((rq, NB), f32),
            pltpu.VMEM((z - 1, rz, NB), f32),
            pltpu.VMEM((total, NB), f32),
            pltpu.VMEM((z, groups, rc, k), f32),
            pltpu.VMEM((groups, z, rc, k), f32),
            pltpu.VMEM((groups - 1, z, rc, k), f32),
            pltpu.VMEM((z, rc, k), f32),
            pltpu.VMEM((z - 1, rc, k), f32),
            pltpu.VMEM((nb, NB, k), f32),
            pltpu.VMEM((nb, NB, k), f32),
            pltpu.VMEM((nb, NB, NB), f32),
            pltpu.VMEM((NB, 2 * NB), f32),
            pltpu.SemaphoreType.DMA((copies,)),
            pltpu.SemaphoreType.DMA((copies,)),
        ],
        compiler_params=pltpu.CompilerParams(
            vmem_limit_bytes=56 << 20, collective_id=0, has_side_effects=True
        ),
    )(owner_perm, packed, centered, parts)


def tdot(a, b):
    return lax.dot_general(a, b, (((0,), (0,)), ((), ())), preferred_element_type=jnp.float32)


def body(groups, devs, dosage, allele_freq, probes, owner_perm):
    mean_dose = 2.0 * allele_freq
    inv_spread = 1.0 / jnp.sqrt(2.0 * allele_freq * (1.0 - allele_freq))
    centered = ((dosage.astype(jnp.float32) - mean_dose[None, :]) * inv_spread[None, :]).astype(
        jnp.bfloat16
    )
    sketch = jnp.dot(centered, probes, preferred_element_type=jnp.float32)
    rounded = lax.reduce_precision(sketch, 8, 7)
    high = rounded.astype(jnp.bfloat16)
    low = (sketch - rounded).astype(jnp.bfloat16)
    local_gram = tdot(high, high) + (tdot(high, low) + tdot(low, high))
    parts = jnp.concatenate([high, low], axis=1)
    return reduce_and_apply(local_gram, centered, parts, owner_perm, groups, devs)


def solution(mesh):
    return jax.shard_map(
        lambda *args: body(mesh.shape["cohort"], mesh.shape["dev"], *args),
        mesh=mesh,
        in_specs=(P(("cohort", "dev"), None), P(), P(), P()),
        out_specs=P("dev", None),
        check_vma=False,
    )
```
